256 devices in a mesh: strip: 32 (over y, x, core), frame: 8 (over z).
Axes of the slice: x: 4, y: 4, z: 8, core: 2. Of those that a mesh axis runs over, the one named last changes fastest.
Arguments:
- estimate: float32 [4096, 2048], P('strip'), may hold values from -6 to 6
- observed: float32 [16, 4096, 2048], P('frame', 'strip'), may hold values from -6 to 6
- weights: float32 [16, 4096, 2048], P('frame', 'strip'), may hold values from 0.3 to 9, as said below
- column_kernels: float32 [16, 65], P('frame'), may hold values from 0.05 to 1
- row_kernels: float32 [16, 65], P('frame'), may hold values from 0.05 to 1
Outputs:
- solution: float32 [4096, 2048], P('strip')
- residual: float32 [4096, 2048], P('strip')
The draws below stay inside these ranges and needn't reach their ends.
Inputs may be any that keep to these rules, and one draw needn't show every extreme that they name: Positive weights of each pixel.
All inputs are finite; a program needn't handle non-finite values.
Results may differ from the reference program's by a relative error of at most 0.00013.
Values sent between devices are 32-bit elements; how exact they have to be, the bound alone decides.
A program may use at most 128 MiB of HBM per device.

```python
import math
import jax
import jax.numpy as jnp
from jax import lax

NC = 2048
TAPS = 65
ITERS = 2
NR = 4096
FRAMES = 16


def draw_weights(key, part):
    base = jnp.exp(jax.random.uniform(key, (FRAMES, NR, NC), jnp.float32, math.log(0.3), math.log(3.0)))
    rising = 3.0 ** (jnp.arange(NR).astype(jnp.float32) / NR)
    return base * rising[None, :, None]


def levels(key, extent, split, least, top_value):
    loudness = 1.0
    for dim, shards_of in split:
        steps = jax.random.uniform(jax.random.fold_in(jax.random.fold_in(key, 6), dim), (shards_of,), jnp.float32, least / len(split), top_value / len(split))
        loudness = loudness * jnp.repeat(jnp.exp(steps), extent[dim] // shards_of).reshape((-1,) + (1,) * (len(extent) - 1 - dim))
    return loudness


def normal_values(own_key, dims, scale, limit, split=(), kind=jnp.bfloat16):
    values = jax.random.normal(own_key, dims, jnp.float32) * scale
    if len(split) > 0:
        values = levels(own_key, dims, split, -0.22, 0.18) * values
    return jnp.clip(values, min=-limit, max=limit).astype(kind)


def setup_inputs(seed: int = 0) -> dict:
    key_of = jax.random.split(jax.random.key(seed), 6)
    estimate = normal_values(key_of[0], (NR, NC), 1.0, 6.0, ((0, 32),), jnp.float32)
    observed = normal_values(key_of[1], (FRAMES, NR, NC), 1.0, 6.0, ((0, 8), (1, 32)), jnp.float32)
    weights = draw_weights(jax.random.fold_in(key_of[5], 71), 0)
    column_kernels = jnp.clip(jnp.exp(math.log(1.0) - 2.9957323 * jax.random.uniform(key_of[3], (FRAMES, TAPS), jnp.float32) ** levels(key_of[3], (FRAMES, TAPS), ((0, 8),), -0.2, 0.2)), 0.05, 1.0)
    row_kernels = jnp.clip(jnp.exp(math.log(1.0) - 2.9957323 * jax.random.uniform(key_of[4], (FRAMES, TAPS), jnp.float32) ** levels(key_of[4], (FRAMES, TAPS), ((0, 8),), -0.2, 0.2)), 0.05, 1.0)
    return {"estimate": estimate, "observed": observed, "weights": weights, "column_kernels": column_kernels, "row_kernels": row_kernels}


damping = 0.05
highest = lax.Precision.HIGHEST


def unit_kernels(kernels):
    return kernels / jnp.sum(kernels, axis=1, keepdims=True)


def single_band(kernel):
    width = kernel.shape[0]
    offset = jnp.arange(256)[:, None] - jnp.arange(128)[None, :] - (width // 2)
    onehot = (offset[:, :, None] == jnp.arange(width)[None, None, :]).astype(jnp.float32)
    return jnp.einsum("amt,t->am", onehot, kernel, precision=highest)


def conv_last(values_in, kernel):
    length = values_in.shape[-1]
    blocks = length // 128
    padded = jnp.pad(values_in, ((0, 0), (64, 64)))
    left_part = padded[:, :length].reshape(values_in.shape[0], blocks, 128)
    right_part = padded[:, 128:length + 128].reshape(values_in.shape[0], blocks, 128)
    window = jnp.concatenate([left_part, right_part], axis=-1)
    result = jnp.einsum("rna,am->rnm", window, single_band(kernel), precision=highest)
    return result.reshape(values_in.shape)


def forward(image, col_kernel, row_kernel):
    spread = conv_last(image, col_kernel)
    return conv_last(spread.T, row_kernel).T


def backward(values_in, col_kernel, row_kernel):
    rows_back = conv_last(values_in.T, row_kernel[::-1]).T
    return conv_last(rows_back, col_kernel[::-1])


def reference(estimate, observed, weights, column_kernels, row_kernels):
    col_unit = unit_kernels(column_kernels)
    row_unit = unit_kernels(row_kernels)

    def normal(image, factor):
        def one_frame(total, items):
            col_kernel, row_kernel, weight_now, observed_now = items
            misfit = forward(image, col_kernel, row_kernel) - factor * observed_now
            return total + backward(weight_now * misfit, col_kernel, row_kernel), None

        total, unused = lax.scan(one_frame, jnp.zeros_like(image), (col_unit, row_unit, weights, observed))
        return total

    solution = estimate
    residual = -(normal(estimate, 1.0) + damping * estimate)
    direction = residual
    norm_now = jnp.sum(residual * residual)
    for iteration in range(ITERS):
        image = normal(direction, 0.0) + damping * direction
        alpha = norm_now / jnp.sum(direction * image)
        solution = solution + alpha * direction
        residual = residual - alpha * image
        norm_next = jnp.sum(residual * residual)
        direction = residual + (norm_next / norm_now) * direction
        norm_now = norm_next
    return solution, residual
```

```python
import functools

import jax
import jax.numpy as jnp
from jax import lax
from jax.experimental import pallas as pl
from jax.experimental.pallas import tpu as pltpu
from jax.sharding import PartitionSpec as P

MESH = pl.DeviceIdType.MESH
damping = 0.05
G = 4
BPG = 16 // G
H = 32
ROWS = 128
EXT = ROWS + 2 * H
Z = 8
PIECE = ROWS // Z
APPLIES = 3
f32, bf16 = jnp.float32, jnp.bfloat16

PARENT = {4: 3, 2: 1, 5: 6, 3: 0, 1: 0, 6: 0, 7: 0}


def children(d):
    return [c for c in PARENT if PARENT[c] == d]


def height(d):
    return 1 + max([height(c) for c in children(d)], default=0)


def depth(d):
    return 0 if d == 0 else 1 + depth(PARENT[d])


TOP = height(0) - 1


def flip(d, g):
    return (Z - d) % Z if g % 2 else d


def split_into(hi_ref, lo_ref, v):
    hi_ref[...] = v.astype(bf16)
    lo_ref[...] = (v - hi_ref[...].astype(f32)).astype(bf16)


def mm(a, b):
    return jnp.dot(a, b, preferred_element_type=f32)


def kernel(vec_ref, est_ref, obs_ref, w_ref, sol_ref, res_ref,
           img, part, hbuf, rbuf, xsh, xsl, uh, ul, yh, yl, zh, zl, prt,
           ch, cl, cth, ctl, rfh, rfl, rth, rtl, s1, s2,
           xss, xsr, hss, hsr, rss, rsr, ags, agr, s1s, s1r, s2s, s2r):
    strip = lax.axis_index("strip")
    z = lax.axis_index("frame")
    up, down = lax.rem(strip + 31, 32), lax.rem(strip + 1, 32)
    yid, rid = strip // 8, lax.rem(strip, 8)

    def zof(off):
        return lax.rem(z + off + Z, Z)

    bar = pltpu.get_barrier_semaphore()
    count = 0
    for d in range(1, Z):
        pl.semaphore_signal(bar, inc=1, device_id={"frame": zof(d)}, device_id_type=MESH)
        count += 1
    for d in range(1, 8):
        pl.semaphore_signal(bar, inc=1, device_id={"strip": yid * 8 + lax.rem(rid + d, 8)}, device_id_type=MESH)
        count += 1
    for d in range(1, 4):
        pl.semaphore_signal(bar, inc=1, device_id={"strip": lax.rem(yid + d, 4) * 8 + rid}, device_id_type=MESH)
        count += 1
    for other in (up, down):
        pl.semaphore_signal(bar, inc=1, device_id={"strip": other}, device_id_type=MESH)
        count += 1

    zero = jnp.zeros((EXT, 128), f32)
    for k in range(APPLIES):
        img[k, 0] = zero
        img[k, 17] = zero
    for b in range(16):
        img[0, 1 + b, pl.ds(H, ROWS), :] = est_ref[:, b * 128:(b + 1) * 128]
    for f in range(2):
        yh[f, 0] = jnp.zeros((ROWS, 128), bf16)
        yl[f, 0] = jnp.zeros((ROWS, 128), bf16)
        yh[f, 17] = jnp.zeros((ROWS, 128), bf16)
        yl[f, 17] = jnp.zeros((ROWS, 128), bf16)
        uh[f, pl.ds(EXT, 64), :] = jnp.zeros((64, 256), bf16)
        ul[f, pl.ds(EXT, 64), :] = jnp.zeros((64, 256), bf16)

    pl.semaphore_wait(bar, count)

    def x_copies(k, g):
        out = []
        for side, (other, src, dst) in enumerate(((up, H, H + ROWS), (down, ROWS, 0))):
            out.append(pltpu.make_async_remote_copy(
                src_ref=img.at[k, pl.ds(1 + BPG * g, BPG), pl.ds(src, H)],
                dst_ref=img.at[k, pl.ds(1 + BPG * g, BPG), pl.ds(dst, H)],
                send_sem=xss.at[k, g, side], recv_sem=xsr.at[k, g, side],
                device_id={"strip": other}, device_id_type=MESH))
        return out

    def x_send(k, g):
        for cp in x_copies(k, g):
            cp.start()

    def x_wait(k, g):
        for cp in x_copies(k, g):
            cp.wait_recv()

        @pl.when(strip == 0)
        def _():
            img[k, pl.ds(1 + BPG * g, BPG), pl.ds(0, H)] = jnp.zeros((BPG, H, 128), f32)

        @pl.when(strip == 31)
        def _():
            img[k, pl.ds(1 + BPG * g, BPG), pl.ds(H + ROWS, H)] = jnp.zeros((BPG, H, 128), f32)

    for g in range(G):
        x_send(0, g)

    def toeplitz(v, rows):
        v = jnp.broadcast_to(v, (rows, 256))
        row = lax.broadcasted_iota(jnp.int32, (rows, 256), 0)
        for bit in range(8):
            if (1 << bit) < rows:
                v = jnp.where((row // (1 << bit)) % 2 == 1, pltpu.roll(v, 1 << bit, 1), v)
        return v

    raw = vec_ref[...]
    unit = raw / jnp.sum(raw, axis=1, keepdims=True)
    for f in range(2):
        kc, kr = unit[f:f + 1], unit[2 + f:3 + f]
        half = pl.ds(f * 128, 128)
        split_into(ch.at[:, half], cl.at[:, half], toeplitz(pltpu.roll(kc, 32, 1), ROWS).T)
        split_into(cth.at[f], ctl.at[f], toeplitz(pltpu.roll(kc, 160, 1), 256)[:, :128])
        band = toeplitz(kr, ROWS)
        split_into(rfh.at[f], rfl.at[f], band)
        split_into(rth.at[:, half], rtl.at[:, half], band.T[:EXT])

    high_lanes = lax.broadcasted_iota(jnp.int32, (EXT, 128), 1) >= 64

    def back_columns(m, f, b):
        lh = jnp.concatenate([yh[f, m], yh[f, m + 1]], axis=1)
        ll = jnp.concatenate([yl[f, m], yl[f, m + 1]], axis=1)
        place = (pl.ds(f * 128, 128), pl.ds(b * 128, 128))
        split_into(zh.at[place], zl.at[place], mm(lh, cth[f]) + mm(ll, cth[f]) + mm(lh, ctl[f]))

    def forward(k, t):
        for i in range(3):
            m = 2 * t + i
            v = jnp.where(high_lanes, img[k, m], img[k, m + 1])
            split_into(xsh.at[i], xsl.at[i], pltpu.roll(v, 64, 1))
        for b in range(2):
            wh = jnp.concatenate([xsh[b], xsh[b + 1]], axis=1)
            wl = jnp.concatenate([xsl[b], xsl[b + 1]], axis=1)
            u = mm(wh, ch[...]) + mm(wl, ch[...]) + mm(wh, cl[...])
            for f in range(2):
                place = (f, pl.ds(0, EXT), pl.ds(b * 128, 128))
                split_into(uh.at[place], ul.at[place], u[:, f * 128:(f + 1) * 128])
        factor = jnp.where(k == 0, 1.0, 0.0).astype(f32)
        lanes = pl.ds(pl.multiple_of(t * 256, 256), 256)
        for f in range(2):
            blurred = mm(rfh[f], uh[f]) + mm(rfl[f], uh[f]) + mm(rfh[f], ul[f])
            y = w_ref[f, :, lanes] * (blurred - factor * obs_ref[f, :, lanes])
            for b in range(2):
                place = (f, 2 * t + 1 + b)
                split_into(yh.at[place], yl.at[place], y[:, b * 128:(b + 1) * 128])

    def backward(t):
        for f in range(2):
            for b in range(2):
                back_columns(2 * t + b, f, b)
        pp = mm(rth[...], zh[...]) + mm(rtl[...], zh[...]) + mm(rth[...], zl[...])
        prt[2 * t] = pp[:, :128]
        prt[2 * t + 1] = pp[:, 128:]

    def compute(k, g):
        start = jnp.where(g == 0, 0, 2 * g + 1)
        end = jnp.where(g == 3, 8, 2 * g + 3)

        def fore(t, carry):
            forward(k, t)
            return carry

        def back(t, carry):
            backward(t)
            return carry

        lax.fori_loop(start, end, fore, 0)
        lax.fori_loop(start, end, back, 0)

        @pl.when(g == 3)
        def _():
            for f in range(2):
                back_columns(16, f, 0)
            a, b = zh[:, 0:128], zl[:, 0:128]
            prt[16] = mm(rth[...], a) + mm(rtl[...], a) + mm(rth[...], b)

        def out(n, carry):
            part[k, n] = pltpu.roll(jnp.where(high_lanes, prt[n], prt[n + 1]), 64, 1)
            return carry

        lax.fori_loop(BPG * g, BPG * g + BPG, out, 0)
        for cp in h_copies(k, g):
            cp.start()

    def h_copies(k, g):
        out = []
        for side, (other, src) in enumerate(((up, 0), (down, H + ROWS))):
            out.append(pltpu.make_async_remote_copy(
                src_ref=part.at[k, pl.ds(BPG * g, BPG), pl.ds(src, H)],
                dst_ref=hbuf.at[k, side, pl.ds(BPG * g, BPG)],
                send_sem=hss.at[k, g, side], recv_sem=hsr.at[k, g, side],
                device_id={"strip": other}, device_id_type=MESH))
        return out

    def h_add(k, g):
        for cp in h_copies(k, g):
            cp.wait_recv()
        blocks = pl.ds(BPG * g, BPG)
        low = jnp.where(strip == 31, 0.0, hbuf[k, 0, blocks])
        part[k, blocks, pl.ds(ROWS, H)] = part[k, blocks, pl.ds(ROWS, H)] + low
        high = jnp.where(strip == 0, 0.0, hbuf[k, 1, blocks])
        part[k, blocks, pl.ds(H, H)] = part[k, blocks, pl.ds(H, H)] + high

    def piece_rows(off):
        return pl.ds(pl.multiple_of(H + PIECE * zof(off), PIECE), PIECE)

    def rs_copy(k, g, d):
        me, to = flip(d, g), flip(PARENT[d], g)
        rows = piece_rows(-me)
        return pltpu.make_async_remote_copy(
            src_ref=part.at[k, pl.ds(BPG * g, BPG), rows],
            dst_ref=rbuf.at[k, d - 1, pl.ds(BPG * g, BPG)],
            send_sem=rss.at[k, g, d - 1], recv_sem=rsr.at[k, g, d - 1],
            device_id={"frame": zof(to - me)}, device_id_type=MESH)

    def rs_level(k, g, level):
        for d in PARENT:
            if height(d) != level:
                continue
            rows = piece_rows(-flip(d, g))
            for c in children(d):
                rs_copy(k, g, c).wait_recv()
                part[k, pl.ds(BPG * g, BPG), rows] = (
                    part[k, pl.ds(BPG * g, BPG), rows] + rbuf[k, c - 1, pl.ds(BPG * g, BPG)])
            rs_copy(k, g, d).start()

    def ag_copy(k, g, d):
        me, to = flip(PARENT[d], g), flip(d, g)
        rows = piece_rows(-me)
        place = img.at[k + 1, pl.ds(1 + BPG * g, BPG), rows]
        return pltpu.make_async_remote_copy(
            src_ref=place, dst_ref=place,
            send_sem=ags.at[k, g, d - 1], recv_sem=agr.at[k, g, d - 1],
            device_id={"frame": zof(to - me)}, device_id_type=MESH)

    def finish_piece(k, g):
        rows = piece_rows(0)
        blocks = pl.ds(BPG * g, BPG)
        total = part[k, blocks, rows]
        for c in children(0):
            rs_copy(k, g, c).wait_recv()
            total = total + rbuf[k, c - 1, blocks]
        inside = pl.ds(1 + BPG * g, BPG)
        total = total + damping * img[k, inside, rows]
        sign = jnp.where(k == 0, -1.0, 1.0).astype(f32)
        img[k + 1, inside, rows] = sign * total
        for c in children(0):
            ag_copy(k, g, c).start()

    def ag_level(k, g, level):
        for d in PARENT:
            if depth(d) != level:
                continue
            ag_copy(k, g, d).wait_recv()
            for c in children(d):
                ag_copy(k, g, c).start()

    def run(item, k, g):
        if item == "H":
            h_add(k, g)
            rs_level(k, g, 1)
        elif item[0] == "R":
            level = int(item[1])
            if level < TOP:
                rs_level(k, g, level + 1)
            else:
                finish_piece(k, g)
        elif item[0] == "A":
            ag_level(k, g, int(item[1]))

    def s1_copy(r, o):
        return pltpu.make_async_remote_copy(
            src_ref=s1.at[r, rid], dst_ref=s1.at[r, rid],
            send_sem=s1s.at[r, o - 1], recv_sem=s1r.at[r, o - 1],
            device_id={"strip": yid * 8 + lax.rem(rid + o, 8)}, device_id_type=MESH)

    def s2_copy(r, o):
        return pltpu.make_async_remote_copy(
            src_ref=s2.at[r, yid], dst_ref=s2.at[r, yid],
            send_sem=s2s.at[r, o - 1], recv_sem=s2r.at[r, o - 1],
            device_id={"strip": lax.rem(yid + o, 4) * 8 + rid}, device_id_type=MESH)

    own = pl.ds(H, ROWS)

    def tiles(v):
        return jnp.sum(v.reshape(ROWS // 8, 8, 128), axis=0)

    def dots(r, fn, count):
        def one(b, c):
            return tuple(x + tiles(v) for x, v in zip(c, fn(b)))
        sums = lax.fori_loop(0, 16, one, tuple(jnp.zeros((8, 128), f32) for _ in range(count)))
        for i in range(2):
            s1[r, rid, pl.ds(8 * i, 8)] = sums[i % count]
        for o in range(1, 8):
            s1_copy(r, o).start()

    def dots_more(r):
        for o in range(1, 8):
            s1_copy(r, o).wait_recv()
        s2[r, yid] = jnp.sum(s1[r], axis=0)
        for o in range(1, 4):
            s2_copy(r, o).start()

    def dots_wait(r):
        for o in range(1, 4):
            s2_copy(r, o).wait_recv()

    def total(r, i):
        return jnp.sum(jnp.sum(s2[r], axis=0)[8 * i:8 * i + 8])

    def rq(b):
        r, q = img[1, 1 + b, own], img[2, 1 + b, own]
        return r * r, r * q

    def rr(alpha0):
        def fn(b):
            r1 = img[1, 1 + b, own] - alpha0 * img[2, 1 + b, own]
            return (r1 * r1,)
        return fn

    stages = ["H"] + [f"R{i}" for i in range(1, TOP + 1)] + [f"A{i}" for i in range(1, TOP + 1)] + ["X"]
    PERIOD = 3 + len(stages) - 1
    table = sorted((g + 2 + i, g, i) for g in range(G) for i in range(len(stages)))

    def act(k, g, i):
        if stages[i] == "X":
            @pl.when(k < APPLIES - 1)
            def _():
                x_wait(k + 1, g)
        else:
            run(stages[i], k, g)
            if stages[i] == f"A{TOP}":
                @pl.when(k < APPLIES - 1)
                def _():
                    x_send(k + 1, g)

    for g in range(G):
        x_wait(0, g)

    def slot(s, carry):
        k, p = s // PERIOD, lax.rem(s, PERIOD)
        for at in range(PERIOD):
            now = [(g, i) for when, g, i in table if when == at]
            late = [(g, i) for when, g, i in table if when == at + PERIOD]
            if late:
                @pl.when((p == at) & (k > 0))
                def _(late=late):
                    for g, i in late:
                        act(k - 1, g, i)
            if now:
                @pl.when(p == at)
                def _(now=now):
                    for g, i in now:
                        act(k, g, i)

        @pl.when(s == 2 * PERIOD + 2)
        def _():
            dots(0, rq, 2)

        @pl.when(s == 2 * PERIOD + 4)
        def _():
            dots_more(0)

        @pl.when(s == 2 * PERIOD + 5)
        def _():
            dots_wait(0)
            dots(1, rr(total(0, 0) / total(0, 1)), 1)

        @pl.when(s == 2 * PERIOD + 6)
        def _():
            dots_more(1)

        @pl.when(p < G)
        def _():
            compute(k, p)
        return carry

    lax.fori_loop(0, PERIOD * APPLIES, slot, 0)
    for when, g, i in table:
        if when >= PERIOD and stages[i] != "X":
            run(stages[i], APPLIES - 1, g)
    dots_wait(1)
    norm0, curv0, norm1 = total(0, 0), total(0, 1), total(1, 0)
    alpha0 = norm0 / curv0
    beta = norm1 / norm0

    def dm(b):
        r, q, s = img[1, 1 + b, own], img[2, 1 + b, own], img[3, 1 + b, own]
        d1 = (r - alpha0 * q) + beta * r
        return (d1 * ((1.0 + beta) * q - alpha0 * s),)

    dots(2, dm, 1)
    dots_more(2)
    dots_wait(2)
    alpha1 = norm1 / total(2, 0)

    def last(b, c):
        e, r, q, s = img[0, 1 + b, own], img[1, 1 + b, own], img[2, 1 + b, own], img[3, 1 + b, own]
        r1 = r - alpha0 * q
        d1 = r1 + beta * r
        image = (1.0 + beta) * q - alpha0 * s
        lanes = pl.ds(pl.multiple_of(b * 128, 128), 128)
        sol_ref[:, lanes] = e + alpha0 * r + alpha1 * d1
        res_ref[:, lanes] = r1 - alpha1 * image
        return c

    lax.fori_loop(0, 16, last, 0)

    def done(k, c):
        for g in range(G):
            for cp in x_copies(k, g) + h_copies(k, g):
                cp.wait_send()
            for d in PARENT:
                rs_copy(k, g, d).wait_send()
                ag_copy(k, g, d).wait_send()
        return c

    lax.fori_loop(0, APPLIES, done, 0)
    for r in range(3):
        for o in range(1, 8):
            s1_copy(r, o).wait_send()
        for o in range(1, 4):
            s2_copy(r, o).wait_send()


def body(estimate, observed, weights, column_kernels, row_kernels):
    vec = jnp.pad(jnp.concatenate([column_kernels, row_kernels]), ((0, 0), (0, 256 - 65)))
    vm = pl.BlockSpec(memory_space=pltpu.VMEM)
    dma = pltpu.SemaphoreType.DMA
    K = APPLIES
    return tuple(pl.pallas_call(
        kernel,
        out_shape=[jax.ShapeDtypeStruct(estimate.shape, f32)] * 2,
        in_specs=[vm] * 4,
        out_specs=[vm] * 2,
        scratch_shapes=[
            pltpu.VMEM((K + 1, 18, EXT, 128), f32),
            pltpu.VMEM((K, 16, EXT, 128), f32),
            pltpu.VMEM((K, 2, 16, H, 128), f32),
            pltpu.VMEM((K, Z - 1, 16, PIECE, 128), f32),
            pltpu.VMEM((3, EXT, 128), bf16),
            pltpu.VMEM((3, EXT, 128), bf16),
            pltpu.VMEM((2, 256, 256), bf16),
            pltpu.VMEM((2, 256, 256), bf16),
            pltpu.VMEM((2, 18, ROWS, 128), bf16),
            pltpu.VMEM((2, 18, ROWS, 128), bf16),
            pltpu.VMEM((256, 256), bf16),
            pltpu.VMEM((256, 256), bf16),
            pltpu.VMEM((17, EXT, 128), f32),
            pltpu.VMEM((256, 256), bf16),
            pltpu.VMEM((256, 256), bf16),
            pltpu.VMEM((2, 256, 128), bf16),
            pltpu.VMEM((2, 256, 128), bf16),
            pltpu.VMEM((2, ROWS, 256), bf16),
            pltpu.VMEM((2, ROWS, 256), bf16),
            pltpu.VMEM((EXT, 256), bf16),
            pltpu.VMEM((EXT, 256), bf16),
            pltpu.VMEM((3, 8, 16, 128), f32),
            pltpu.VMEM((3, 4, 16, 128), f32),
            dma((K, G, 2)), dma((K, G, 2)),
            dma((K, G, 2)), dma((K, G, 2)),
            dma((K, G, Z - 1)), dma((K, G, Z - 1)),
            dma((K, G, Z - 1)), dma((K, G, Z - 1)),
            dma((3, 7)), dma((3, 7)),
            dma((3, 3)), dma((3, 3)),
        ],
        compiler_params=pltpu.CompilerParams(
            collective_id=0, has_side_effects=True, vmem_limit_bytes=48 << 20),
        cost_estimate=pl.CostEstimate(flops=13_000_000_000, bytes_accessed=8_000_000, transcendentals=0),
    )(vec, estimate, observed, weights))


def solution(mesh):
    return jax.shard_map(
        body,
        mesh=mesh,
        in_specs=(
            P("strip", None),
            P("frame", "strip", None),
            P("frame", "strip", None),
            P("frame", None),
            P("frame", None),
        ),
        out_specs=(P("strip", None), P("strip", None)),
        check_vma=False,
    )
```

```python
import functools

import jax
import jax.numpy as jnp
from jax import lax
from jax.experimental import pallas as pl
from jax.experimental.pallas import tpu as pltpu
from jax.sharding import PartitionSpec as P

MESH = pl.DeviceIdType.MESH
damping = 0.05
G = 4
BPG = 16 // G
H = 32
ROWS = 128
EXT = ROWS + 2 * H
Z = 8
PIECE = ROWS // Z
APPLIES = 3
f32, bf16 = jnp.float32, jnp.bfloat16

PARENT = {4: 2, 3: 2, 5: 6, 2: 0, 1: 0, 6: 0, 7: 0}


def children(d):
    return [c for c in PARENT if PARENT[c] == d]


def height(d):
    return 1 + max([height(c) for c in children(d)], default=0)


def depth(d):
    return 0 if d == 0 else 1 + depth(PARENT[d])


TOP = height(0) - 1


def flip(d, g):
    return (Z - d) % Z if g % 2 else d


def split_into(hi_ref, lo_ref, v):
    hi_ref[...] = v.astype(bf16)
    lo_ref[...] = (v - hi_ref[...].astype(f32)).astype(bf16)


def mm(a, b):
    return jnp.dot(a, b, preferred_element_type=f32)


def kernel(vec_ref, est_ref, obs_hbm, w_hbm, sol_ref, res_ref,
           img, part, hbuf, rbuf, xsh, xsl, uh, ul, yh, yl, zh, zl, prt,
           ch, cl, cth, ctl, rfh, rfl, rth, rtl, s1, s2, s0, obs_ref, w_ref, blur, ld, s0s, s0r,
           xss, xsr, hss, hsr, rss, rsr, ags, agr, s1s, s1r, s2s, s2r):
    strip = lax.axis_index("strip")
    z = lax.axis_index("frame")
    up, down = lax.rem(strip + 31, 32), lax.rem(strip + 1, 32)
    yid, rid = strip // 8, lax.rem(strip, 8)

    zs = [lax.rem(z + d, Z) for d in range(Z)]
    starts = [H + PIECE * v for v in zs]
    peers8 = [yid * 8 + lax.rem(rid + d, 8) for d in range(8)]
    peers4 = [lax.rem(yid + d, 4) * 8 + rid for d in range(4)]

    def zof(off):
        return zs[off % Z]

    loads = [pltpu.make_async_copy(obs_hbm, obs_ref, ld.at[0]), pltpu.make_async_copy(w_hbm, w_ref, ld.at[1])]
    for cp in loads:
        cp.start()

    bar = pltpu.get_barrier_semaphore()
    count = 0
    for d in range(1, Z):
        pl.semaphore_signal(bar, inc=1, device_id={"frame": zof(d)}, device_id_type=MESH)
        count += 1
    for d in range(1, 8):
        pl.semaphore_signal(bar, inc=1, device_id={"strip": peers8[d]}, device_id_type=MESH)
        count += 1
    for d in range(1, 4):
        pl.semaphore_signal(bar, inc=1, device_id={"strip": peers4[d]}, device_id_type=MESH)
        count += 1
    for other in (up, down):
        pl.semaphore_signal(bar, inc=1, device_id={"strip": other}, device_id_type=MESH)
        count += 1

    zero = jnp.zeros((EXT, 128), f32)
    for k in range(APPLIES):
        img[k, 0] = zero
        img[k, 17] = zero
    for b in range(16):
        img[0, 1 + b, pl.ds(H, ROWS), :] = est_ref[:, b * 128:(b + 1) * 128]
    for f in range(2):
        yh[f, 0] = jnp.zeros((ROWS, 128), bf16)
        yl[f, 0] = jnp.zeros((ROWS, 128), bf16)
        yh[f, 17] = jnp.zeros((ROWS, 128), bf16)
        yl[f, 17] = jnp.zeros((ROWS, 128), bf16)
        uh[f, pl.ds(EXT, 64), :] = jnp.zeros((64, 256), bf16)
        ul[f, pl.ds(EXT, 64), :] = jnp.zeros((64, 256), bf16)

    pl.semaphore_wait(bar, count)

    def x_copies(k, g):
        out = []
        for side, (other, src, dst) in enumerate(((up, H, H + ROWS), (down, ROWS, 0))):
            out.append(pltpu.make_async_remote_copy(
                src_ref=img.at[k, pl.ds(1 + BPG * g, BPG), pl.ds(src, H)],
                dst_ref=img.at[k, pl.ds(1 + BPG * g, BPG), pl.ds(dst, H)],
                send_sem=xss.at[k, g, side], recv_sem=xsr.at[k, g, side],
                device_id={"strip": other}, device_id_type=MESH))
        return out

    def x_send(k, g):
        for cp in x_copies(k, g):
            cp.start()

    def x_wait(k, g):
        for cp in x_copies(k, g):
            cp.wait_recv()

        @pl.when(strip == 0)
        def _():
            img[k, pl.ds(1 + BPG * g, BPG), pl.ds(0, H)] = jnp.zeros((BPG, H, 128), f32)

        @pl.when(strip == 31)
        def _():
            img[k, pl.ds(1 + BPG * g, BPG), pl.ds(H + ROWS, H)] = jnp.zeros((BPG, H, 128), f32)

    for g in range(G):
        x_send(0, g)

    def toeplitz(v, rows):
        v = jnp.broadcast_to(v, (rows, 256))
        row = lax.broadcasted_iota(jnp.int32, (rows, 256), 0)
        for bit in range(8):
            if (1 << bit) < rows:
                v = jnp.where((row // (1 << bit)) % 2 == 1, pltpu.roll(v, 1 << bit, 1), v)
        return v

    raw = vec_ref[...]
    unit = raw / jnp.sum(raw, axis=1, keepdims=True)
    for f in range(2):
        kc, kr = unit[f:f + 1], unit[2 + f:3 + f]
        half = pl.ds(f * 128, 128)
        split_into(ch.at[:, half], cl.at[:, half], toeplitz(pltpu.roll(kc, 32, 1), ROWS).T)
        split_into(cth.at[f], ctl.at[f], toeplitz(pltpu.roll(kc, 160, 1), 256)[:, :128])
        band = toeplitz(kr, ROWS)
        split_into(rfh.at[f], rfl.at[f], band)
        split_into(rth.at[:, half], rtl.at[:, half], band.T[:EXT])

    high_lanes = lax.broadcasted_iota(jnp.int32, (EXT, 128), 1) >= 64

    def back_columns(m, f, b):
        lh = jnp.concatenate([yh[f, m], yh[f, m + 1]], axis=1)
        ll = jnp.concatenate([yl[f, m], yl[f, m + 1]], axis=1)
        place = (pl.ds(f * 128, 128), pl.ds(b * 128, 128))
        split_into(zh.at[place], zl.at[place], mm(lh, cth[f]) + mm(ll, cth[f]) + mm(lh, ctl[f]))

    def forward(k, t):
        for i in range(3):
            m = 2 * t + i
            v = jnp.where(high_lanes, img[k, m], img[k, m + 1])
            split_into(xsh.at[i], xsl.at[i], pltpu.roll(v, 64, 1))
        for b in range(2):
            wh = jnp.concatenate([xsh[b], xsh[b + 1]], axis=1)
            wl = jnp.concatenate([xsl[b], xsl[b + 1]], axis=1)
            u = mm(wh, ch[...]) + mm(wl, ch[...]) + mm(wh, cl[...])
            for f in range(2):
                place = (f, pl.ds(0, EXT), pl.ds(b * 128, 128))
                split_into(uh.at[place], ul.at[place], u[:, f * 128:(f + 1) * 128])
        factor = jnp.where(k == 0, 1.0, 0.0).astype(f32)
        lanes = pl.ds(pl.multiple_of(t * 256, 256), 256)
        for f in range(2):
            blurred = mm(rfh[f], uh[f]) + mm(rfl[f], uh[f]) + mm(rfh[f], ul[f])
            blur[k, f, :, lanes] = blurred
            y = w_ref[f, :, lanes] * (blurred - factor * obs_ref[f, :, lanes])
            for b in range(2):
                place = (f, 2 * t + 1 + b)
                split_into(yh.at[place], yl.at[place], y[:, b * 128:(b + 1) * 128])

    def backward(t):
        for f in range(2):
            for b in range(2):
                back_columns(2 * t + b, f, b)
        pp = mm(rth[...], zh[...]) + mm(rtl[...], zh[...]) + mm(rth[...], zl[...])
        prt[2 * t] = pp[:, :128]
        prt[2 * t + 1] = pp[:, 128:]

    def compute(k, g):
        start = jnp.where(g == 0, 0, 2 * g + 1)
        end = jnp.where(g == 3, 8, 2 * g + 3)

        def fore(t, carry):
            forward(k, t)
            return carry

        def back(t, carry):
            backward(t)
            return carry

        lax.fori_loop(start, end, fore, 0)
        lax.fori_loop(start, end, back, 0)

        @pl.when(g == 3)
        def _():
            for f in range(2):
                back_columns(16, f, 0)
            a, b = zh[:, 0:128], zl[:, 0:128]
            prt[16] = mm(rth[...], a) + mm(rtl[...], a) + mm(rth[...], b)

        def out(n, carry):
            part[k, n] = pltpu.roll(jnp.where(high_lanes, prt[n], prt[n + 1]), 64, 1)
            return carry

        lax.fori_loop(BPG * g, BPG * g + BPG, out, 0)
        for cp in h_copies(k, g):
            cp.start()

    def h_copies(k, g):
        out = []
        for side, (other, src) in enumerate(((up, 0), (down, H + ROWS))):
            out.append(pltpu.make_async_remote_copy(
                src_ref=part.at[k, pl.ds(BPG * g, BPG), pl.ds(src, H)],
                dst_ref=hbuf.at[k, side, pl.ds(BPG * g, BPG)],
                send_sem=hss.at[k, g, side], recv_sem=hsr.at[k, g, side],
                device_id={"strip": other}, device_id_type=MESH))
        return out

    def h_add(k, g):
        for cp in h_copies(k, g):
            cp.wait_recv()
        blocks = pl.ds(BPG * g, BPG)
        low = jnp.where(strip == 31, 0.0, hbuf[k, 0, blocks])
        part[k, blocks, pl.ds(ROWS, H)] = part[k, blocks, pl.ds(ROWS, H)] + low
        high = jnp.where(strip == 0, 0.0, hbuf[k, 1, blocks])
        part[k, blocks, pl.ds(H, H)] = part[k, blocks, pl.ds(H, H)] + high

    def piece_rows(off):
        return pl.ds(pl.multiple_of(starts[off % Z], PIECE), PIECE)

    def rs_copy(k, g, d):
        me, to = flip(d, g), flip(PARENT[d], g)
        rows = piece_rows(-me)
        return pltpu.make_async_remote_copy(
            src_ref=part.at[k, pl.ds(BPG * g, BPG), rows],
            dst_ref=rbuf.at[k, d - 1, pl.ds(BPG * g, BPG)],
            send_sem=rss.at[k, g, d - 1], recv_sem=rsr.at[k, g, d - 1],
            device_id={"frame": zof(to - me)}, device_id_type=MESH)

    def rs_level(k, g, level):
        for d in PARENT:
            if height(d) != level:
                continue
            rows = piece_rows(-flip(d, g))
            for c in children(d):
                rs_copy(k, g, c).wait_recv()
                part[k, pl.ds(BPG * g, BPG), rows] = (
                    part[k, pl.ds(BPG * g, BPG), rows] + rbuf[k, c - 1, pl.ds(BPG * g, BPG)])
            rs_copy(k, g, d).start()

    def ag_copy(k, g, d):
        me, to = flip(PARENT[d], g), flip(d, g)
        rows = piece_rows(-me)
        place = img.at[k + 1, pl.ds(1 + BPG * g, BPG), rows]
        return pltpu.make_async_remote_copy(
            src_ref=place, dst_ref=place,
            send_sem=ags.at[k, g, d - 1], recv_sem=agr.at[k, g, d - 1],
            device_id={"frame": zof(to - me)}, device_id_type=MESH)

    def finish_piece(k, g):
        rows = piece_rows(0)
        blocks = pl.ds(BPG * g, BPG)
        total = part[k, blocks, rows]
        for c in children(0):
            rs_copy(k, g, c).wait_recv()
            total = total + rbuf[k, c - 1, blocks]
        inside = pl.ds(1 + BPG * g, BPG)
        total = total + damping * img[k, inside, rows]
        sign = jnp.where(k == 0, -1.0, 1.0).astype(f32)
        img[k + 1, inside, rows] = sign * total
        for c in children(0):
            ag_copy(k, g, c).start()

    def ag_level(k, g, level):
        for d in PARENT:
            if depth(d) != level:
                continue
            ag_copy(k, g, d).wait_recv()
            for c in children(d):
                ag_copy(k, g, c).start()

    def run(item, k, g):
        if item == "H":
            h_add(k, g)
            rs_level(k, g, 1)
        elif item[0] == "R":
            level = int(item[1])
            if level < TOP:
                rs_level(k, g, level + 1)
            else:
                finish_piece(k, g)
        elif item[0] == "A":
            ag_level(k, g, int(item[1]))

    def s1_copy(r, o):
        return pltpu.make_async_remote_copy(
            src_ref=s1.at[r, rid], dst_ref=s1.at[r, rid],
            send_sem=s1s.at[r, o - 1], recv_sem=s1r.at[r, o - 1],
            device_id={"strip": peers8[o]}, device_id_type=MESH)

    def s2_copy(r, o):
        return pltpu.make_async_remote_copy(
            src_ref=s2.at[r, yid], dst_ref=s2.at[r, yid],
            send_sem=s2s.at[r, o - 1], recv_sem=s2r.at[r, o - 1],
            device_id={"strip": peers4[o]}, device_id_type=MESH)

    own = pl.ds(H, ROWS)

    def tiles(v):
        return jnp.sum(v.reshape(ROWS // 8, 8, 128), axis=0)

    def dots(r, fn, count):
        def one(b, c):
            return tuple(x + tiles(v) for x, v in zip(c, fn(b)))
        sums = lax.fori_loop(0, 16, one, tuple(jnp.zeros((8, 128), f32) for _ in range(count)))
        dots_send(r, [sums[i % count] for i in range(2)])

    def dots_send(r, sums):
        for i in range(2):
            s1[r, rid, pl.ds(8 * i, 8)] = sums[i]
        for o in range(1, 8):
            s1_copy(r, o).start()

    def dots_more(r):
        for o in range(1, 8):
            s1_copy(r, o).wait_recv()
        s2[r, yid] = jnp.sum(s1[r], axis=0)
        for o in range(1, 4):
            s2_copy(r, o).start()

    def dots_wait(r):
        for o in range(1, 4):
            s2_copy(r, o).wait_recv()

    def total(r, i):
        return jnp.sum(jnp.sum(s2[r], axis=0)[8 * i:8 * i + 8])

    def rq(b):
        r, q = img[1, 1 + b, own], img[2, 1 + b, own]
        return r * r, r * q

    def rr(alpha0):
        def fn(b):
            r1 = img[1, 1 + b, own] - alpha0 * img[2, 1 + b, own]
            return (r1 * r1,)
        return fn

    def s0_copy(o):
        return pltpu.make_async_remote_copy(
            src_ref=s0.at[z], dst_ref=s0.at[z],
            send_sem=s0s.at[o - 1], recv_sem=s0r.at[o - 1],
            device_id={"frame": zof(o)}, device_id_type=MESH)

    def coefficients():
        norm0, curv0, norm1 = total(0, 0), total(0, 1), total(1, 0)
        return norm0 / curv0, norm1 / norm0, norm1

    def curvature_part():
        alpha0, beta, _ = coefficients()

        def one(b, c):
            lanes = pl.ds(pl.multiple_of(b * 128, 128), 128)
            r, q = img[1, 1 + b, own], img[2, 1 + b, own]
            d1 = (r - alpha0 * q) + beta * r
            v = (damping / Z) * (d1 * d1)
            for f in range(2):
                a, m = blur[1, f, :, lanes], blur[2, f, :, lanes]
                a = (a - alpha0 * m) + beta * a
                v = v + w_ref[f, :, lanes] * (a * a)
            return c + tiles(v)

        s0[z] = lax.fori_loop(0, 16, one, jnp.zeros((8, 128), f32))

    stages = ["H"] + [f"R{i}" for i in range(1, TOP + 1)] + [f"A{i}" for i in range(1, TOP + 1)] + ["X"]
    PERIOD = 3 + len(stages) - 1
    table = sorted(((g + 2 + i, g, i) for g in range(G) for i in range(len(stages))), key=lambda e: (e[0], -e[1]))

    def act(k, g, i):
        if stages[i] == "X":
            @pl.when(k < APPLIES - 1)
            def _():
                x_wait(k + 1, g)
        else:
            run(stages[i], k, g)
            if stages[i] == f"A{TOP}":
                @pl.when(k < APPLIES - 1)
                def _():
                    x_send(k + 1, g)

    for g in range(G):
        x_wait(0, g)
    for cp in loads:
        cp.wait()

    def slot(s, carry):
        k, p = s // PERIOD, lax.rem(s, PERIOD)
        for at in range(PERIOD):
            now = [(g, i) for when, g, i in table if when == at]
            late = [(g, i) for when, g, i in table if when == at + PERIOD]
            if late:
                @pl.when((p == at) & (k > 0))
                def _(late=late):
                    for g, i in late:
                        act(k - 1, g, i)
            if now:
                @pl.when(p == at)
                def _(now=now):
                    for g, i in now:
                        act(k, g, i)

        @pl.when(s == 2 * PERIOD + 2)
        def _():
            dots(0, rq, 2)

        @pl.when(s == 2 * PERIOD + 3)
        def _():
            dots_more(0)

        @pl.when(s == 2 * PERIOD + 4)
        def _():
            dots_wait(0)
            dots(1, rr(total(0, 0) / total(0, 1)), 1)

        @pl.when(s == 2 * PERIOD + 5)
        def _():
            dots_more(1)

        @pl.when(s == 2 * PERIOD + 6)
        def _():
            dots_wait(1)
            curvature_part()
            for o in range(1, Z):
                s0_copy(o).start()

        @pl.when(s == 2 * PERIOD + 7)
        def _():
            for o in range(1, Z):
                s0_copy(o).wait_recv()
            v = jnp.sum(s0[...], axis=0)
            dots_send(2, [v, v])

        @pl.when(p < G)
        def _():
            compute(k, p)
        return carry

    lax.fori_loop(0, PERIOD * APPLIES, slot, 0)
    steps = sorted({when for when, g, i in table if when >= PERIOD and stages[i] != "X"})
    for n, step in enumerate(steps):
        for when, g, i in table:
            if when == step and stages[i] != "X":
                run(stages[i], APPLIES - 1, g)
        if n == 0:
            dots_more(2)
    dots_wait(2)
    alpha0, beta, norm1 = coefficients()
    alpha1 = norm1 / total(2, 0)

    def last(b, c):
        e, r, q, s = img[0, 1 + b, own], img[1, 1 + b, own], img[2, 1 + b, own], img[3, 1 + b, own]
        r1 = r - alpha0 * q
        d1 = r1 + beta * r
        image = (1.0 + beta) * q - alpha0 * s
        lanes = pl.ds(pl.multiple_of(b * 128, 128), 128)
        sol_ref[:, lanes] = e + alpha0 * r + alpha1 * d1
        res_ref[:, lanes] = r1 - alpha1 * image
        return c

    lax.fori_loop(0, 16, last, 0)

    for o in range(1, Z):
        s0_copy(o).wait_send()
    def done(k, c):
        for g in range(G):
            for cp in x_copies(k, g) + h_copies(k, g):
                cp.wait_send()
            for d in PARENT:
                rs_copy(k, g, d).wait_send()
                ag_copy(k, g, d).wait_send()
        return c

    lax.fori_loop(0, APPLIES, done, 0)
    for r in range(3):
        for o in range(1, 8):
            s1_copy(r, o).wait_send()
        for o in range(1, 4):
            s2_copy(r, o).wait_send()


def body(estimate, observed, weights, column_kernels, row_kernels):
    vec = jnp.pad(jnp.concatenate([column_kernels, row_kernels]), ((0, 0), (0, 256 - 65)))
    vm = pl.BlockSpec(memory_space=pltpu.VMEM)
    dma = pltpu.SemaphoreType.DMA
    K = APPLIES
    return tuple(pl.pallas_call(
        kernel,
        out_shape=[jax.ShapeDtypeStruct(estimate.shape, f32)] * 2,
        in_specs=[vm, vm, pl.BlockSpec(memory_space=pl.ANY), pl.BlockSpec(memory_space=pl.ANY)],
        out_specs=[vm] * 2,
        scratch_shapes=[
            pltpu.VMEM((K + 1, 18, EXT, 128), f32),
            pltpu.VMEM((K, 16, EXT, 128), f32),
            pltpu.VMEM((K, 2, 16, H, 128), f32),
            pltpu.VMEM((K, Z - 1, 16, PIECE, 128), f32),
            pltpu.VMEM((3, EXT, 128), bf16),
            pltpu.VMEM((3, EXT, 128), bf16),
            pltpu.VMEM((2, 256, 256), bf16),
            pltpu.VMEM((2, 256, 256), bf16),
            pltpu.VMEM((2, 18, ROWS, 128), bf16),
            pltpu.VMEM((2, 18, ROWS, 128), bf16),
            pltpu.VMEM((256, 256), bf16),
            pltpu.VMEM((256, 256), bf16),
            pltpu.VMEM((17, EXT, 128), f32),
            pltpu.VMEM((256, 256), bf16),
            pltpu.VMEM((256, 256), bf16),
            pltpu.VMEM((2, 256, 128), bf16),
            pltpu.VMEM((2, 256, 128), bf16),
            pltpu.VMEM((2, ROWS, 256), bf16),
            pltpu.VMEM((2, ROWS, 256), bf16),
            pltpu.VMEM((EXT, 256), bf16),
            pltpu.VMEM((EXT, 256), bf16),
            pltpu.VMEM((3, 8, 16, 128), f32),
            pltpu.VMEM((3, 4, 16, 128), f32),
            pltpu.VMEM((8, 8, 128), f32),
            pltpu.VMEM((2, ROWS, 2048), f32),
            pltpu.VMEM((2, ROWS, 2048), f32),
            pltpu.VMEM((K, 2, ROWS, 2048), f32),
            dma((2,)), dma((7,)), dma((7,)),
            dma((K, G, 2)), dma((K, G, 2)),
            dma((K, G, 2)), dma((K, G, 2)),
            dma((K, G, Z - 1)), dma((K, G, Z - 1)),
            dma((K, G, Z - 1)), dma((K, G, Z - 1)),
            dma((3, 7)), dma((3, 7)),
            dma((3, 3)), dma((3, 3)),
        ],
        compiler_params=pltpu.CompilerParams(
            collective_id=0, has_side_effects=True, vmem_limit_bytes=48 << 20),
        cost_estimate=pl.CostEstimate(flops=13_000_000_000, bytes_accessed=8_000_000, transcendentals=0),
    )(vec, estimate, observed, weights))


def solution(mesh):
    return jax.shard_map(
        body,
        mesh=mesh,
        in_specs=(
            P("strip", None),
            P("frame", "strip", None),
            P("frame", "strip", None),
            P("frame", None),
            P("frame", None),
        ),
        out_specs=(P("strip", None), P("strip", None)),
        check_vma=False,
    )
```

```python
import functools

import jax
import jax.numpy as jnp
from jax import lax
from jax.experimental import pallas as pl
from jax.experimental.pallas import tpu as pltpu
from jax.sharding import PartitionSpec as P

MESH = pl.DeviceIdType.MESH
damping = 0.05
G = 4
BPG = 16 // G
H = 32
ROWS = 128
EXT = ROWS + 2 * H
Z = 8
PIECE = ROWS // Z
APPLIES = 3
f32, bf16 = jnp.float32, jnp.bfloat16

PARENT = {4: 2, 3: 2, 5: 6, 2: 0, 1: 0, 6: 0, 7: 0}


def children(d):
    return [c for c in PARENT if PARENT[c] == d]


def height(d):
    return 1 + max([height(c) for c in children(d)], default=0)


def depth(d):
    return 0 if d == 0 else 1 + depth(PARENT[d])


TOP = height(0) - 1


def flip(d, g):
    return (Z - d) % Z if g % 2 else d


def split_into(hi_ref, lo_ref, v):
    hi_ref[...] = v.astype(bf16)
    lo_ref[...] = (v - hi_ref[...].astype(f32)).astype(bf16)


def mm(a, b):
    return jnp.dot(a, b, preferred_element_type=f32)


def kernel(vec_ref, est_ref, obs_hbm, w_hbm, sol_ref, res_ref,
           img, part, hbuf, rbuf, xsh, xsl, uh, ul, yh, yl, zh, zl, prt,
           ch, cl, cth, ctl, rfh, rfl, rth, rtl, s1, s2, s0, obs_ref, w_ref, blur, ld, s0s, s0r,
           xss, xsr, hss, hsr, rss, rsr, ags, agr, s1s, s1r, s2s, s2r):
    strip = lax.axis_index("strip")
    z = lax.axis_index("frame")
    up, down = lax.rem(strip + 31, 32), lax.rem(strip + 1, 32)
    yid, rid = strip // 8, lax.rem(strip, 8)

    zs = [lax.rem(z + d, Z) for d in range(Z)]
    starts = [H + PIECE * v for v in zs]
    peers8 = [yid * 8 + lax.rem(rid + d, 8) for d in range(8)]
    peers4 = [lax.rem(yid + d, 4) * 8 + rid for d in range(4)]

    def zof(off):
        return zs[off % Z]

    def arrived(sem, ref):
        pltpu.make_async_copy(ref, ref, sem).wait()

    def pieces(n):
        return part.at[0, pl.ds(0, BPG), pl.ds(0, PIECE * n)]

    loads = [pltpu.make_async_copy(obs_hbm, obs_ref, ld.at[0]), pltpu.make_async_copy(w_hbm, w_ref, ld.at[1])]
    for cp in loads:
        cp.start()

    bar = pltpu.get_barrier_semaphore()
    count = 0
    for d in range(1, Z):
        pl.semaphore_signal(bar, inc=1, device_id={"frame": zof(d)}, device_id_type=MESH)
        count += 1
    for d in range(1, 8):
        pl.semaphore_signal(bar, inc=1, device_id={"strip": peers8[d]}, device_id_type=MESH)
        count += 1
    for d in range(1, 4):
        pl.semaphore_signal(bar, inc=1, device_id={"strip": peers4[d]}, device_id_type=MESH)
        count += 1
    for other in (up, down):
        pl.semaphore_signal(bar, inc=1, device_id={"strip": other}, device_id_type=MESH)
        count += 1

    zero = jnp.zeros((EXT, 128), f32)
    for k in range(APPLIES):
        img[k, 0] = zero
        img[k, 17] = zero
    for b in range(16):
        img[0, 1 + b, pl.ds(H, ROWS), :] = est_ref[:, b * 128:(b + 1) * 128]
    for f in range(2):
        yh[f, 0] = jnp.zeros((ROWS, 128), bf16)
        yl[f, 0] = jnp.zeros((ROWS, 128), bf16)
        yh[f, 17] = jnp.zeros((ROWS, 128), bf16)
        yl[f, 17] = jnp.zeros((ROWS, 128), bf16)
        uh[f, pl.ds(EXT, 64), :] = jnp.zeros((64, 256), bf16)
        ul[f, pl.ds(EXT, 64), :] = jnp.zeros((64, 256), bf16)

    pl.semaphore_wait(bar, count)

    def x_copies(k, g):
        out = []
        for side, (other, src, dst) in enumerate(((up, H, H + ROWS), (down, ROWS, 0))):
            out.append(pltpu.make_async_remote_copy(
                src_ref=img.at[k, pl.ds(1 + BPG * g, BPG), pl.ds(src, H)],
                dst_ref=img.at[k, pl.ds(1 + BPG * g, BPG), pl.ds(dst, H)],
                send_sem=xss.at[k], recv_sem=xsr.at[k, g],
                device_id={"strip": other}, device_id_type=MESH))
        return out

    def x_send(k, g):
        for cp in x_copies(k, g):
            cp.start()

    def x_wait(k, g):
        arrived(xsr.at[k, g], pieces(2 * 2 * H // (2 * PIECE)))

        @pl.when(strip == 0)
        def _():
            img[k, pl.ds(1 + BPG * g, BPG), pl.ds(0, H)] = jnp.zeros((BPG, H, 128), f32)

        @pl.when(strip == 31)
        def _():
            img[k, pl.ds(1 + BPG * g, BPG), pl.ds(H + ROWS, H)] = jnp.zeros((BPG, H, 128), f32)

    for g in range(G):
        x_send(0, g)

    def toeplitz(v, rows):
        v = jnp.broadcast_to(v, (rows, 256))
        row = lax.broadcasted_iota(jnp.int32, (rows, 256), 0)
        for bit in range(8):
            if (1 << bit) < rows:
                v = jnp.where((row // (1 << bit)) % 2 == 1, pltpu.roll(v, 1 << bit, 1), v)
        return v

    raw = vec_ref[...]
    unit = raw / jnp.sum(raw, axis=1, keepdims=True)
    for f in range(2):
        kc, kr = unit[f:f + 1], unit[2 + f:3 + f]
        half = pl.ds(f * 128, 128)
        split_into(ch.at[:, half], cl.at[:, half], toeplitz(pltpu.roll(kc, 32, 1), ROWS).T)
        split_into(cth.at[f], ctl.at[f], toeplitz(pltpu.roll(kc, 160, 1), 256)[:, :128])
        band = toeplitz(kr, ROWS)
        split_into(rfh.at[f], rfl.at[f], band)
        split_into(rth.at[:, half], rtl.at[:, half], band.T[:EXT])

    high_lanes = lax.broadcasted_iota(jnp.int32, (EXT, 128), 1) >= 64

    def back_columns(m, f, b):
        lh = jnp.concatenate([yh[f, m], yh[f, m + 1]], axis=1)
        ll = jnp.concatenate([yl[f, m], yl[f, m + 1]], axis=1)
        place = (pl.ds(f * 128, 128), pl.ds(b * 128, 128))
        split_into(zh.at[place], zl.at[place], mm(lh, cth[f]) + mm(ll, cth[f]) + mm(lh, ctl[f]))

    def forward(k, t):
        for i in range(3):
            m = 2 * t + i
            v = jnp.where(high_lanes, img[k, m], img[k, m + 1])
            split_into(xsh.at[i], xsl.at[i], pltpu.roll(v, 64, 1))
        for b in range(2):
            wh = jnp.concatenate([xsh[b], xsh[b + 1]], axis=1)
            wl = jnp.concatenate([xsl[b], xsl[b + 1]], axis=1)
            u = mm(wh, ch[...]) + mm(wl, ch[...]) + mm(wh, cl[...])
            for f in range(2):
                place = (f, pl.ds(0, EXT), pl.ds(b * 128, 128))
                split_into(uh.at[place], ul.at[place], u[:, f * 128:(f + 1) * 128])
        factor = jnp.where(k == 0, 1.0, 0.0).astype(f32)
        lanes = pl.ds(pl.multiple_of(t * 256, 256), 256)
        for f in range(2):
            blurred = mm(rfh[f], uh[f]) + mm(rfl[f], uh[f]) + mm(rfh[f], ul[f])
            blur[k, f, :, lanes] = blurred
            y = w_ref[f, :, lanes] * (blurred - factor * obs_ref[f, :, lanes])
            for b in range(2):
                place = (f, 2 * t + 1 + b)
                split_into(yh.at[place], yl.at[place], y[:, b * 128:(b + 1) * 128])

    def backward(t):
        for f in range(2):
            for b in range(2):
                back_columns(2 * t + b, f, b)
        pp = mm(rth[...], zh[...]) + mm(rtl[...], zh[...]) + mm(rth[...], zl[...])
        prt[2 * t] = pp[:, :128]
        prt[2 * t + 1] = pp[:, 128:]

    def compute(k, g):
        start = jnp.where(g == 0, 0, 2 * g + 1)
        end = jnp.where(g == 3, 8, 2 * g + 3)

        def fore(t, carry):
            forward(k, t)
            return carry

        def back(t, carry):
            backward(t)
            return carry

        lax.fori_loop(start, end, fore, 0)
        lax.fori_loop(start, end, back, 0)

        @pl.when(g == 3)
        def _():
            for f in range(2):
                back_columns(16, f, 0)
            a, b = zh[:, 0:128], zl[:, 0:128]
            prt[16] = mm(rth[...], a) + mm(rtl[...], a) + mm(rth[...], b)

        def out(n, carry):
            part[k, n] = pltpu.roll(jnp.where(high_lanes, prt[n], prt[n + 1]), 64, 1)
            return carry

        lax.fori_loop(BPG * g, BPG * g + BPG, out, 0)
        for cp in h_copies(k, g):
            cp.start()

    def h_copies(k, g):
        out = []
        for side, (other, src) in enumerate(((up, 0), (down, H + ROWS))):
            out.append(pltpu.make_async_remote_copy(
                src_ref=part.at[k, pl.ds(BPG * g, BPG), pl.ds(src, H)],
                dst_ref=hbuf.at[k, side, pl.ds(BPG * g, BPG)],
                send_sem=hss.at[k], recv_sem=hsr.at[k, g],
                device_id={"strip": other}, device_id_type=MESH))
        return out

    def h_add(k, g):
        arrived(hsr.at[k, g], pieces(2 * 2 * H // (2 * PIECE)))
        blocks = pl.ds(BPG * g, BPG)
        low = jnp.where(strip == 31, 0.0, hbuf[k, 0, blocks])
        part[k, blocks, pl.ds(ROWS, H)] = part[k, blocks, pl.ds(ROWS, H)] + low
        high = jnp.where(strip == 0, 0.0, hbuf[k, 1, blocks])
        part[k, blocks, pl.ds(H, H)] = part[k, blocks, pl.ds(H, H)] + high

    def piece_rows(off):
        return pl.ds(pl.multiple_of(starts[off % Z], PIECE), PIECE)

    def rs_copy(k, g, d):
        me, to = flip(d, g), flip(PARENT[d], g)
        rows = piece_rows(-me)
        return pltpu.make_async_remote_copy(
            src_ref=part.at[k, pl.ds(BPG * g, BPG), rows],
            dst_ref=rbuf.at[k, d - 1, pl.ds(BPG * g, BPG)],
            send_sem=rss.at[k], recv_sem=rsr.at[k, g, PARENT[d]],
            device_id={"frame": zof(to - me)}, device_id_type=MESH)

    def rs_level(k, g, level):
        for d in PARENT:
            if height(d) != level:
                continue
            rows = piece_rows(-flip(d, g))
            if children(d):
                arrived(rsr.at[k, g, d], pieces(len(children(d))))
            for c in children(d):
                part[k, pl.ds(BPG * g, BPG), rows] = (
                    part[k, pl.ds(BPG * g, BPG), rows] + rbuf[k, c - 1, pl.ds(BPG * g, BPG)])
            rs_copy(k, g, d).start()

    def ag_copy(k, g, d):
        me, to = flip(PARENT[d], g), flip(d, g)
        rows = piece_rows(-me)
        place = img.at[k + 1, pl.ds(1 + BPG * g, BPG), rows]
        return pltpu.make_async_remote_copy(
            src_ref=place, dst_ref=place,
            send_sem=ags.at[k], recv_sem=agr.at[k, g, d if children(d) else 0],
            device_id={"frame": zof(to - me)}, device_id_type=MESH)

    def finish_piece(k, g):
        rows = piece_rows(0)
        blocks = pl.ds(BPG * g, BPG)
        total = part[k, blocks, rows]
        arrived(rsr.at[k, g, 0], pieces(len(children(0))))
        for c in children(0):
            total = total + rbuf[k, c - 1, blocks]
        inside = pl.ds(1 + BPG * g, BPG)
        total = total + damping * img[k, inside, rows]
        sign = jnp.where(k == 0, -1.0, 1.0).astype(f32)
        img[k + 1, inside, rows] = sign * total
        for c in children(0):
            ag_copy(k, g, c).start()

    def ag_level(k, g, level):
        for d in PARENT:
            if depth(d) != level or not children(d):
                continue
            arrived(agr.at[k, g, d], pieces(1))
            for c in children(d):
                ag_copy(k, g, c).start()
        if level == TOP:
            arrived(agr.at[k, g, 0], pieces(len([d for d in PARENT if not children(d)])))

    def run(item, k, g):
        if item == "H":
            h_add(k, g)
            rs_level(k, g, 1)
        elif item[0] == "R":
            level = int(item[1])
            if level < TOP:
                rs_level(k, g, level + 1)
            else:
                finish_piece(k, g)
        elif item[0] == "A":
            ag_level(k, g, int(item[1]))

    def s1_copy(r, o):
        return pltpu.make_async_remote_copy(
            src_ref=s1.at[r, rid], dst_ref=s1.at[r, rid],
            send_sem=s1s.at[r], recv_sem=s1r.at[r],
            device_id={"strip": peers8[o]}, device_id_type=MESH)

    def s2_copy(r, o):
        return pltpu.make_async_remote_copy(
            src_ref=s2.at[r, yid], dst_ref=s2.at[r, yid],
            send_sem=s2s.at[r], recv_sem=s2r.at[r],
            device_id={"strip": peers4[o]}, device_id_type=MESH)

    own = pl.ds(H, ROWS)

    def tiles(v):
        return jnp.sum(v.reshape(ROWS // 8, 8, 128), axis=0)

    def dots(r, fn, count):
        def one(b, c):
            return tuple(x + tiles(v) for x, v in zip(c, fn(b)))
        sums = lax.fori_loop(0, 16, one, tuple(jnp.zeros((8, 128), f32) for _ in range(count)))
        dots_send(r, [sums[i % count] for i in range(2)])

    def dots_send(r, sums):
        for i in range(2):
            s1[r, rid, pl.ds(8 * i, 8)] = sums[i]
        for o in range(1, 8):
            s1_copy(r, o).start()

    def dots_more(r):
        arrived(s1r.at[r], s1.at[r, pl.ds(0, 7)])
        s2[r, yid] = jnp.sum(s1[r], axis=0)
        for o in range(1, 4):
            s2_copy(r, o).start()

    def dots_wait(r):
        arrived(s2r.at[r], s2.at[r, pl.ds(0, 3)])

    def total(r, i):
        return jnp.sum(jnp.sum(s2[r], axis=0)[8 * i:8 * i + 8])

    def rq(b):
        r, q = img[1, 1 + b, own], img[2, 1 + b, own]
        return r * r, r * q

    def rr(alpha0):
        def fn(b):
            r1 = img[1, 1 + b, own] - alpha0 * img[2, 1 + b, own]
            return (r1 * r1,)
        return fn

    def s0_copy(o):
        return pltpu.make_async_remote_copy(
            src_ref=s0.at[z], dst_ref=s0.at[z],
            send_sem=s0s.at[0], recv_sem=s0r.at[0],
            device_id={"frame": zof(o)}, device_id_type=MESH)

    def coefficients():
        norm0, curv0, norm1 = total(0, 0), total(0, 1), total(1, 0)
        return norm0 / curv0, norm1 / norm0, norm1

    def curvature_part():
        alpha0, beta, _ = coefficients()

        def one(b, c):
            lanes = pl.ds(pl.multiple_of(b * 128, 128), 128)
            r, q = img[1, 1 + b, own], img[2, 1 + b, own]
            d1 = (r - alpha0 * q) + beta * r
            v = (damping / Z) * (d1 * d1)
            for f in range(2):
                a, m = blur[1, f, :, lanes], blur[2, f, :, lanes]
                a = (a - alpha0 * m) + beta * a
                v = v + w_ref[f, :, lanes] * (a * a)
            return c + tiles(v)

        s0[z] = lax.fori_loop(0, 16, one, jnp.zeros((8, 128), f32))

    stages = ["H"] + [f"R{i}" for i in range(1, TOP + 1)] + [f"A{i}" for i in range(1, TOP + 1)] + ["X"]
    PERIOD = 3 + len(stages) - 1
    table = sorted(((g + 2 + i, g, i) for g in range(G) for i in range(len(stages))), key=lambda e: (e[0], -e[1]))

    def act(k, g, i):
        if stages[i] == "X":
            @pl.when(k < APPLIES - 1)
            def _():
                x_wait(k + 1, g)
        else:
            run(stages[i], k, g)
            if stages[i] == f"A{TOP}":
                @pl.when(k < APPLIES - 1)
                def _():
                    x_send(k + 1, g)

    for g in range(G):
        x_wait(0, g)
    for cp in loads:
        cp.wait()

    def slot(s, carry):
        k, p = s // PERIOD, lax.rem(s, PERIOD)
        for at in range(PERIOD):
            now = [(g, i) for when, g, i in table if when == at]
            late = [(g, i) for when, g, i in table if when == at + PERIOD]
            if late:
                @pl.when((p == at) & (k > 0))
                def _(late=late):
                    for g, i in late:
                        act(k - 1, g, i)
            if now:
                @pl.when(p == at)
                def _(now=now):
                    for g, i in now:
                        act(k, g, i)

        @pl.when(s == 2 * PERIOD + 2)
        def _():
            dots(0, rq, 2)

        @pl.when(s == 2 * PERIOD + 3)
        def _():
            dots_more(0)

        @pl.when(s == 2 * PERIOD + 4)
        def _():
            dots_wait(0)
            dots(1, rr(total(0, 0) / total(0, 1)), 1)

        @pl.when(s == 2 * PERIOD + 5)
        def _():
            dots_more(1)

        @pl.when(s == 2 * PERIOD + 6)
        def _():
            dots_wait(1)
            curvature_part()
            for o in range(1, Z):
                s0_copy(o).start()

        @pl.when(s == 2 * PERIOD + 7)
        def _():
            arrived(s0r.at[0], s0.at[pl.ds(0, 7)])
            v = jnp.sum(s0[...], axis=0)
            dots_send(2, [v, v])

        @pl.when(p < G)
        def _():
            compute(k, p)
        return carry

    lax.fori_loop(0, PERIOD * APPLIES, slot, 0)
    steps = sorted({when for when, g, i in table if when >= PERIOD and stages[i] != "X"})
    for n, step in enumerate(steps):
        for when, g, i in table:
            if when == step and stages[i] != "X":
                run(stages[i], APPLIES - 1, g)
        if n == 0:
            dots_more(2)
    dots_wait(2)
    alpha0, beta, norm1 = coefficients()
    alpha1 = norm1 / total(2, 0)

    def last(b, c):
        e, r, q, s = img[0, 1 + b, own], img[1, 1 + b, own], img[2, 1 + b, own], img[3, 1 + b, own]
        r1 = r - alpha0 * q
        d1 = r1 + beta * r
        image = (1.0 + beta) * q - alpha0 * s
        lanes = pl.ds(pl.multiple_of(b * 128, 128), 128)
        sol_ref[:, lanes] = e + alpha0 * r + alpha1 * d1
        res_ref[:, lanes] = r1 - alpha1 * image
        return c

    lax.fori_loop(0, 16, last, 0)

    for k in range(APPLIES):
        arrived(xss.at[k], hbuf.at[k])
        arrived(hss.at[k], hbuf.at[k])
        arrived(rss.at[k], rbuf.at[k])
        arrived(ags.at[k], rbuf.at[k])
    for r in range(3):
        arrived(s1s.at[r], s1.at[r, pl.ds(0, 7)])
        arrived(s2s.at[r], s2.at[r, pl.ds(0, 3)])
    arrived(s0s.at[0], s0.at[pl.ds(0, 7)])


def body(estimate, observed, weights, column_kernels, row_kernels):
    vec = jnp.pad(jnp.concatenate([column_kernels, row_kernels]), ((0, 0), (0, 256 - 65)))
    vm = pl.BlockSpec(memory_space=pltpu.VMEM)
    dma = pltpu.SemaphoreType.DMA
    K = APPLIES
    return tuple(pl.pallas_call(
        kernel,
        out_shape=[jax.ShapeDtypeStruct(estimate.shape, f32)] * 2,
        in_specs=[vm, vm, pl.BlockSpec(memory_space=pl.ANY), pl.BlockSpec(memory_space=pl.ANY)],
        out_specs=[vm] * 2,
        scratch_shapes=[
            pltpu.VMEM((K + 1, 18, EXT, 128), f32),
            pltpu.VMEM((K, 16, EXT, 128), f32),
            pltpu.VMEM((K, 2, 16, H, 128), f32),
            pltpu.VMEM((K, Z - 1, 16, PIECE, 128), f32),
            pltpu.VMEM((3, EXT, 128), bf16),
            pltpu.VMEM((3, EXT, 128), bf16),
            pltpu.VMEM((2, 256, 256), bf16),
            pltpu.VMEM((2, 256, 256), bf16),
            pltpu.VMEM((2, 18, ROWS, 128), bf16),
            pltpu.VMEM((2, 18, ROWS, 128), bf16),
            pltpu.VMEM((256, 256), bf16),
            pltpu.VMEM((256, 256), bf16),
            pltpu.VMEM((17, EXT, 128), f32),
            pltpu.VMEM((256, 256), bf16),
            pltpu.VMEM((256, 256), bf16),
            pltpu.VMEM((2, 256, 128), bf16),
            pltpu.VMEM((2, 256, 128), bf16),
            pltpu.VMEM((2, ROWS, 256), bf16),
            pltpu.VMEM((2, ROWS, 256), bf16),
            pltpu.VMEM((EXT, 256), bf16),
            pltpu.VMEM((EXT, 256), bf16),
            pltpu.VMEM((3, 8, 16, 128), f32),
            pltpu.VMEM((3, 4, 16, 128), f32),
            pltpu.VMEM((8, 8, 128), f32),
            pltpu.VMEM((2, ROWS, 2048), f32),
            pltpu.VMEM((2, ROWS, 2048), f32),
            pltpu.VMEM((K, 2, ROWS, 2048), f32),
            dma((2,)), dma((1,)), dma((1,)),
            dma((K,)), dma((K, G)),
            dma((K,)), dma((K, G)),
            dma((K,)), dma((K, G, Z)),
            dma((K,)), dma((K, G, Z)),
            dma((3,)), dma((3,)),
            dma((3,)), dma((3,)),
        ],
        compiler_params=pltpu.CompilerParams(
            collective_id=0, has_side_effects=True, vmem_limit_bytes=48 << 20),
        cost_estimate=pl.CostEstimate(flops=13_000_000_000, bytes_accessed=8_000_000, transcendentals=0),
    )(vec, estimate, observed, weights))


def solution(mesh):
    return jax.shard_map(
        body,
        mesh=mesh,
        in_specs=(
            P("strip", None),
            P("frame", "strip", None),
            P("frame", "strip", None),
            P("frame", None),
            P("frame", None),
        ),
        out_specs=(P("strip", None), P("strip", None)),
        check_vma=False,
    )
```

```python
import functools

import jax
import jax.numpy as jnp
from jax import lax
from jax.experimental import pallas as pl
from jax.experimental.pallas import tpu as pltpu
from jax.sharding import PartitionSpec as P

MESH = pl.DeviceIdType.MESH
damping = 0.05
G = 4
BPG = 16 // G
H = 32
ROWS = 128
EXT = ROWS + 2 * H
Z = 8
PIECE = ROWS // Z
APPLIES = 3
f32, bf16 = jnp.float32, jnp.bfloat16

PARENT = {4: 3, 3: 2, 5: 6, 6: 7, 2: 0, 1: 0, 7: 0}


def children(d):
    return [c for c in PARENT if PARENT[c] == d]


def height(d):
    return 1 + max([height(c) for c in children(d)], default=0)


def depth(d):
    return 0 if d == 0 else 1 + depth(PARENT[d])


TOP = height(0) - 1


def flip(d, g):
    return (Z - d) % Z if g % 2 else d


def split_into(hi_ref, lo_ref, v):
    hi_ref[...] = v.astype(bf16)
    lo_ref[...] = (v - hi_ref[...].astype(f32)).astype(bf16)


def mm(a, b):
    return jnp.dot(a, b, preferred_element_type=f32)


def kernel(vec_ref, est_ref, obs_hbm, w_hbm, sol_ref, res_ref,
           img, part, hbuf, rbuf, xsh, xsl, uh, ul, yh, yl, zh, zl, prt,
           ch, cl, cth, ctl, rfh, rfl, rth, rtl, s1, s2, s0, obs_ref, w_ref, blur, ld, s0s, s0r,
           xss, xsr, hss, hsr, rss, rsr, ags, agr, s1s, s1r, s2s, s2r):
    strip = lax.axis_index("strip")
    z = lax.axis_index("frame")
    up, down = lax.rem(strip + 31, 32), lax.rem(strip + 1, 32)
    yid, rid = strip // 8, lax.rem(strip, 8)

    zs = [lax.rem(z + d, Z) for d in range(Z)]
    starts = [H + PIECE * v for v in zs]
    peers8 = [yid * 8 + lax.rem(rid + d, 8) for d in range(8)]
    peers4 = [lax.rem(yid + d, 4) * 8 + rid for d in range(4)]

    def zof(off):
        return zs[off % Z]

    def arrived(sem, ref):
        pltpu.make_async_copy(ref, ref, sem).wait()

    def pieces(n):
        return part.at[0, pl.ds(0, BPG), pl.ds(0, PIECE * n)]

    loads = [pltpu.make_async_copy(obs_hbm, obs_ref, ld.at[0]), pltpu.make_async_copy(w_hbm, w_ref, ld.at[1])]
    for cp in loads:
        cp.start()

    bar = pltpu.get_barrier_semaphore()
    count = 0
    for d in range(1, Z):
        pl.semaphore_signal(bar, inc=1, device_id={"frame": zof(d)}, device_id_type=MESH)
        count += 1
    for d in range(1, 8):
        pl.semaphore_signal(bar, inc=1, device_id={"strip": peers8[d]}, device_id_type=MESH)
        count += 1
    for d in range(1, 4):
        pl.semaphore_signal(bar, inc=1, device_id={"strip": peers4[d]}, device_id_type=MESH)
        count += 1
    for other in (up, down):
        pl.semaphore_signal(bar, inc=1, device_id={"strip": other}, device_id_type=MESH)
        count += 1

    zero = jnp.zeros((EXT, 128), f32)
    for k in range(APPLIES):
        img[k, 0] = zero
        img[k, 17] = zero
    for b in range(16):
        img[0, 1 + b, pl.ds(H, ROWS), :] = est_ref[:, b * 128:(b + 1) * 128]
    for f in range(2):
        yh[f, 0] = jnp.zeros((ROWS, 128), bf16)
        yl[f, 0] = jnp.zeros((ROWS, 128), bf16)
        yh[f, 17] = jnp.zeros((ROWS, 128), bf16)
        yl[f, 17] = jnp.zeros((ROWS, 128), bf16)
        uh[f, pl.ds(EXT, 64), :] = jnp.zeros((64, 256), bf16)
        ul[f, pl.ds(EXT, 64), :] = jnp.zeros((64, 256), bf16)

    pl.semaphore_wait(bar, count)

    def x_copies(k, g):
        out = []
        for side, (other, src, dst) in enumerate(((up, H, H + ROWS), (down, ROWS, 0))):
            out.append(pltpu.make_async_remote_copy(
                src_ref=img.at[k, pl.ds(1 + BPG * g, BPG), pl.ds(src, H)],
                dst_ref=img.at[k, pl.ds(1 + BPG * g, BPG), pl.ds(dst, H)],
                send_sem=xss.at[k], recv_sem=xsr.at[k, g],
                device_id={"strip": other}, device_id_type=MESH))
        return out

    def x_send(k, g):
        for cp in x_copies(k, g):
            cp.start()

    def x_wait(k, g):
        arrived(xsr.at[k, g], pieces(2 * 2 * H // (2 * PIECE)))

        @pl.when(strip == 0)
        def _():
            img[k, pl.ds(1 + BPG * g, BPG), pl.ds(0, H)] = jnp.zeros((BPG, H, 128), f32)

        @pl.when(strip == 31)
        def _():
            img[k, pl.ds(1 + BPG * g, BPG), pl.ds(H + ROWS, H)] = jnp.zeros((BPG, H, 128), f32)

    for g in range(G):
        x_send(0, g)

    def toeplitz(v, rows):
        v = jnp.broadcast_to(v, (rows, 256))
        row = lax.broadcasted_iota(jnp.int32, (rows, 256), 0)
        for bit in range(8):
            if (1 << bit) < rows:
                v = jnp.where((row // (1 << bit)) % 2 == 1, pltpu.roll(v, 1 << bit, 1), v)
        return v

    raw = vec_ref[...]
    unit = raw / jnp.sum(raw, axis=1, keepdims=True)
    for f in range(2):
        kc, kr = unit[f:f + 1], unit[2 + f:3 + f]
        half = pl.ds(f * 128, 128)
        split_into(ch.at[:, half], cl.at[:, half], toeplitz(pltpu.roll(kc, 32, 1), ROWS).T)
        split_into(cth.at[f], ctl.at[f], toeplitz(pltpu.roll(kc, 160, 1), 256)[:, :128])
        band = toeplitz(kr, ROWS)
        split_into(rfh.at[f], rfl.at[f], band)
        split_into(rth.at[:, half], rtl.at[:, half], band.T[:EXT])

    high_lanes = lax.broadcasted_iota(jnp.int32, (EXT, 128), 1) >= 64

    def back_columns(m, f, b):
        lh = jnp.concatenate([yh[f, m], yh[f, m + 1]], axis=1)
        ll = jnp.concatenate([yl[f, m], yl[f, m + 1]], axis=1)
        place = (pl.ds(f * 128, 128), pl.ds(b * 128, 128))
        split_into(zh.at[place], zl.at[place], mm(lh, cth[f]) + mm(ll, cth[f]) + mm(lh, ctl[f]))

    def forward(k, t):
        for i in range(3):
            m = 2 * t + i
            v = jnp.where(high_lanes, img[k, m], img[k, m + 1])
            split_into(xsh.at[i], xsl.at[i], pltpu.roll(v, 64, 1))
        for b in range(2):
            wh = jnp.concatenate([xsh[b], xsh[b + 1]], axis=1)
            wl = jnp.concatenate([xsl[b], xsl[b + 1]], axis=1)
            u = mm(wh, ch[...]) + mm(wl, ch[...]) + mm(wh, cl[...])
            for f in range(2):
                place = (f, pl.ds(0, EXT), pl.ds(b * 128, 128))
                split_into(uh.at[place], ul.at[place], u[:, f * 128:(f + 1) * 128])
        factor = jnp.where(k == 0, 1.0, 0.0).astype(f32)
        lanes = pl.ds(pl.multiple_of(t * 256, 256), 256)
        for f in range(2):
            blurred = mm(rfh[f], uh[f]) + mm(rfl[f], uh[f]) + mm(rfh[f], ul[f])
            blur[k, f, :, lanes] = blurred
            y = w_ref[f, :, lanes] * (blurred - factor * obs_ref[f, :, lanes])
            for b in range(2):
                place = (f, 2 * t + 1 + b)
                split_into(yh.at[place], yl.at[place], y[:, b * 128:(b + 1) * 128])

    def backward(t):
        for f in range(2):
            for b in range(2):
                back_columns(2 * t + b, f, b)
        pp = mm(rth[...], zh[...]) + mm(rtl[...], zh[...]) + mm(rth[...], zl[...])
        prt[2 * t] = pp[:, :128]
        prt[2 * t + 1] = pp[:, 128:]

    def compute(k, g):
        start = jnp.where(g == 0, 0, 2 * g + 1)
        end = jnp.where(g == 3, 8, 2 * g + 3)

        def fore(t, carry):
            forward(k, t)
            return carry

        def back(t, carry):
            backward(t)
            return carry

        lax.fori_loop(start, end, fore, 0)
        lax.fori_loop(start, end, back, 0)

        @pl.when(g == 3)
        def _():
            for f in range(2):
                back_columns(16, f, 0)
            a, b = zh[:, 0:128], zl[:, 0:128]
            prt[16] = mm(rth[...], a) + mm(rtl[...], a) + mm(rth[...], b)

        def out(n, carry):
            part[k, n] = pltpu.roll(jnp.where(high_lanes, prt[n], prt[n + 1]), 64, 1)
            return carry

        lax.fori_loop(BPG * g, BPG * g + BPG, out, 0)
        for cp in h_copies(k, g):
            cp.start()

    def h_copies(k, g):
        out = []
        for side, (other, src) in enumerate(((up, 0), (down, H + ROWS))):
            out.append(pltpu.make_async_remote_copy(
                src_ref=part.at[k, pl.ds(BPG * g, BPG), pl.ds(src, H)],
                dst_ref=hbuf.at[k, side, pl.ds(BPG * g, BPG)],
                send_sem=hss.at[k], recv_sem=hsr.at[k, g],
                device_id={"strip": other}, device_id_type=MESH))
        return out

    def h_add(k, g):
        arrived(hsr.at[k, g], pieces(2 * 2 * H // (2 * PIECE)))
        blocks = pl.ds(BPG * g, BPG)
        low = jnp.where(strip == 31, 0.0, hbuf[k, 0, blocks])
        part[k, blocks, pl.ds(ROWS, H)] = part[k, blocks, pl.ds(ROWS, H)] + low
        high = jnp.where(strip == 0, 0.0, hbuf[k, 1, blocks])
        part[k, blocks, pl.ds(H, H)] = part[k, blocks, pl.ds(H, H)] + high

    def piece_rows(off):
        return pl.ds(pl.multiple_of(starts[off % Z], PIECE), PIECE)

    def rs_copy(k, g, d):
        me, to = flip(d, g), flip(PARENT[d], g)
        rows = piece_rows(-me)
        return pltpu.make_async_remote_copy(
            src_ref=part.at[k, pl.ds(BPG * g, BPG), rows],
            dst_ref=rbuf.at[k, d - 1, pl.ds(BPG * g, BPG)],
            send_sem=rss.at[k], recv_sem=rsr.at[k, g, PARENT[d]],
            device_id={"frame": zof(to - me)}, device_id_type=MESH)

    def rs_level(k, g, level):
        for d in PARENT:
            if height(d) != level:
                continue
            rows = piece_rows(-flip(d, g))
            if children(d):
                arrived(rsr.at[k, g, d], pieces(len(children(d))))
            for c in children(d):
                part[k, pl.ds(BPG * g, BPG), rows] = (
                    part[k, pl.ds(BPG * g, BPG), rows] + rbuf[k, c - 1, pl.ds(BPG * g, BPG)])
            rs_copy(k, g, d).start()

    def ag_copy(k, g, d):
        me, to = flip(PARENT[d], g), flip(d, g)
        rows = piece_rows(-me)
        place = img.at[k + 1, pl.ds(1 + BPG * g, BPG), rows]
        return pltpu.make_async_remote_copy(
            src_ref=place, dst_ref=place,
            send_sem=ags.at[k], recv_sem=agr.at[k, g, d if children(d) else 0],
            device_id={"frame": zof(to - me)}, device_id_type=MESH)

    def finish_piece(k, g):
        rows = piece_rows(0)
        blocks = pl.ds(BPG * g, BPG)
        total = part[k, blocks, rows]
        arrived(rsr.at[k, g, 0], pieces(len(children(0))))
        for c in children(0):
            total = total + rbuf[k, c - 1, blocks]
        inside = pl.ds(1 + BPG * g, BPG)
        total = total + damping * img[k, inside, rows]
        sign = jnp.where(k == 0, -1.0, 1.0).astype(f32)
        img[k + 1, inside, rows] = sign * total
        for c in children(0):
            ag_copy(k, g, c).start()

    def ag_level(k, g, level):
        for d in PARENT:
            if depth(d) != level or not children(d):
                continue
            arrived(agr.at[k, g, d], pieces(1))
            for c in children(d):
                ag_copy(k, g, c).start()
        if level == TOP:
            arrived(agr.at[k, g, 0], pieces(len([d for d in PARENT if not children(d)])))

    def run(item, k, g):
        if item == "H":
            h_add(k, g)
            rs_level(k, g, 1)
        elif item[0] == "R":
            level = int(item[1])
            if level < TOP:
                rs_level(k, g, level + 1)
            else:
                finish_piece(k, g)
        elif item[0] == "A":
            ag_level(k, g, int(item[1]))

    def s1_copy(r, o):
        return pltpu.make_async_remote_copy(
            src_ref=s1.at[r, rid], dst_ref=s1.at[r, rid],
            send_sem=s1s.at[r], recv_sem=s1r.at[r],
            device_id={"strip": peers8[o]}, device_id_type=MESH)

    def s2_copy(r, o):
        return pltpu.make_async_remote_copy(
            src_ref=s2.at[r, yid], dst_ref=s2.at[r, yid],
            send_sem=s2s.at[r], recv_sem=s2r.at[r],
            device_id={"strip": peers4[o]}, device_id_type=MESH)

    own = pl.ds(H, ROWS)

    def tiles(v):
        return jnp.sum(v.reshape(ROWS // 8, 8, 128), axis=0)

    def dots(r, fn, count):
        def one(b, c):
            return tuple(x + tiles(v) for x, v in zip(c, fn(b)))
        sums = lax.fori_loop(0, 16, one, tuple(jnp.zeros((8, 128), f32) for _ in range(count)))
        dots_send(r, [sums[i % count] for i in range(2)])

    def dots_send(r, sums):
        for i in range(2):
            s1[r, rid, pl.ds(8 * i, 8)] = sums[i]
        for o in range(1, 8):
            s1_copy(r, o).start()

    def dots_more(r):
        arrived(s1r.at[r], s1.at[r, pl.ds(0, 7)])
        s2[r, yid] = jnp.sum(s1[r], axis=0)
        for o in range(1, 4):
            s2_copy(r, o).start()

    def dots_wait(r):
        arrived(s2r.at[r], s2.at[r, pl.ds(0, 3)])

    def total(r, i):
        return jnp.sum(jnp.sum(s2[r], axis=0)[8 * i:8 * i + 8])

    def rq(b):
        r, q = img[1, 1 + b, own], img[2, 1 + b, own]
        return r * r, r * q

    def rr(alpha0):
        def fn(b):
            r1 = img[1, 1 + b, own] - alpha0 * img[2, 1 + b, own]
            return (r1 * r1,)
        return fn

    def s0_copy(o):
        return pltpu.make_async_remote_copy(
            src_ref=s0.at[z], dst_ref=s0.at[z],
            send_sem=s0s.at[0], recv_sem=s0r.at[0],
            device_id={"frame": zof(o)}, device_id_type=MESH)

    def coefficients():
        norm0, curv0, norm1 = total(0, 0), total(0, 1), total(1, 0)
        return norm0 / curv0, norm1 / norm0, norm1

    def curvature_part():
        alpha0, beta, _ = coefficients()

        def one(b, c):
            lanes = pl.ds(pl.multiple_of(b * 128, 128), 128)
            r, q = img[1, 1 + b, own], img[2, 1 + b, own]
            d1 = (r - alpha0 * q) + beta * r
            v = (damping / Z) * (d1 * d1)
            for f in range(2):
                a, m = blur[1, f, :, lanes], blur[2, f, :, lanes]
                a = (a - alpha0 * m) + beta * a
                v = v + w_ref[f, :, lanes] * (a * a)
            return c + tiles(v)

        s0[z] = lax.fori_loop(0, 16, one, jnp.zeros((8, 128), f32))

    stages = ["H"] + [f"R{i}" for i in range(1, TOP + 1)] + [f"A{i}" for i in range(1, TOP + 1)] + ["X"]
    PERIOD = 3 + len(stages) - 1
    table = sorted(((g + 2 + i, g, i) for g in range(G) for i in range(len(stages))), key=lambda e: (e[0], -e[1]))

    def act(k, g, i):
        if stages[i] == "X":
            @pl.when(k < APPLIES - 1)
            def _():
                x_wait(k + 1, g)
        else:
            run(stages[i], k, g)
            if stages[i] == f"A{TOP}":
                @pl.when(k < APPLIES - 1)
                def _():
                    x_send(k + 1, g)

    for g in range(G):
        x_wait(0, g)
    for cp in loads:
        cp.wait()

    def slot(s, carry):
        k, p = s // PERIOD, lax.rem(s, PERIOD)
        for at in range(PERIOD):
            now = [(g, i) for when, g, i in table if when == at]
            late = [(g, i) for when, g, i in table if when == at + PERIOD]
            if late:
                @pl.when((p == at) & (k > 0))
                def _(late=late):
                    for g, i in late:
                        act(k - 1, g, i)
            if now:
                @pl.when(p == at)
                def _(now=now):
                    for g, i in now:
                        act(k, g, i)

        @pl.when(s == 2 * PERIOD + 2)
        def _():
            dots(0, rq, 2)

        @pl.when(s == 2 * PERIOD + 3)
        def _():
            dots_more(0)

        @pl.when(s == 2 * PERIOD + 4)
        def _():
            dots_wait(0)
            dots(1, rr(total(0, 0) / total(0, 1)), 1)

        @pl.when(s == 2 * PERIOD + 5)
        def _():
            dots_more(1)

        @pl.when(s == 2 * PERIOD + 6)
        def _():
            dots_wait(1)
            curvature_part()
            for o in range(1, Z):
                s0_copy(o).start()

        @pl.when(s == 2 * PERIOD + 7)
        def _():
            arrived(s0r.at[0], s0.at[pl.ds(0, 7)])
            v = jnp.sum(s0[...], axis=0)
            dots_send(2, [v, v])

        @pl.when(p < G)
        def _():
            compute(k, p)
        return carry

    lax.fori_loop(0, PERIOD * APPLIES, slot, 0)
    steps = sorted({when for when, g, i in table if when >= PERIOD and stages[i] != "X"})
    for n, step in enumerate(steps):
        for when, g, i in table:
            if when == step and stages[i] != "X":
                run(stages[i], APPLIES - 1, g)
        if n == 0:
            dots_more(2)
    dots_wait(2)
    alpha0, beta, norm1 = coefficients()
    alpha1 = norm1 / total(2, 0)

    def last(b, c):
        e, r, q, s = img[0, 1 + b, own], img[1, 1 + b, own], img[2, 1 + b, own], img[3, 1 + b, own]
        r1 = r - alpha0 * q
        d1 = r1 + beta * r
        image = (1.0 + beta) * q - alpha0 * s
        lanes = pl.ds(pl.multiple_of(b * 128, 128), 128)
        sol_ref[:, lanes] = e + alpha0 * r + alpha1 * d1
        res_ref[:, lanes] = r1 - alpha1 * image
        return c

    lax.fori_loop(0, 16, last, 0)

    for k in range(APPLIES):
        arrived(xss.at[k], hbuf.at[k])
        arrived(hss.at[k], hbuf.at[k])
        arrived(rss.at[k], rbuf.at[k])
        arrived(ags.at[k], rbuf.at[k])
    for r in range(3):
        arrived(s1s.at[r], s1.at[r, pl.ds(0, 7)])
        arrived(s2s.at[r], s2.at[r, pl.ds(0, 3)])
    arrived(s0s.at[0], s0.at[pl.ds(0, 7)])


def body(estimate, observed, weights, column_kernels, row_kernels):
    vec = jnp.pad(jnp.concatenate([column_kernels, row_kernels]), ((0, 0), (0, 256 - 65)))
    vm = pl.BlockSpec(memory_space=pltpu.VMEM)
    dma = pltpu.SemaphoreType.DMA
    K = APPLIES
    return tuple(pl.pallas_call(
        kernel,
        out_shape=[jax.ShapeDtypeStruct(estimate.shape, f32)] * 2,
        in_specs=[vm, vm, pl.BlockSpec(memory_space=pl.ANY), pl.BlockSpec(memory_space=pl.ANY)],
        out_specs=[vm] * 2,
        scratch_shapes=[
            pltpu.VMEM((K + 1, 18, EXT, 128), f32),
            pltpu.VMEM((K, 16, EXT, 128), f32),
            pltpu.VMEM((K, 2, 16, H, 128), f32),
            pltpu.VMEM((K, Z - 1, 16, PIECE, 128), f32),
            pltpu.VMEM((3, EXT, 128), bf16),
            pltpu.VMEM((3, EXT, 128), bf16),
            pltpu.VMEM((2, 256, 256), bf16),
            pltpu.VMEM((2, 256, 256), bf16),
            pltpu.VMEM((2, 18, ROWS, 128), bf16),
            pltpu.VMEM((2, 18, ROWS, 128), bf16),
            pltpu.VMEM((256, 256), bf16),
            pltpu.VMEM((256, 256), bf16),
            pltpu.VMEM((17, EXT, 128), f32),
            pltpu.VMEM((256, 256), bf16),
            pltpu.VMEM((256, 256), bf16),
            pltpu.VMEM((2, 256, 128), bf16),
            pltpu.VMEM((2, 256, 128), bf16),
            pltpu.VMEM((2, ROWS, 256), bf16),
            pltpu.VMEM((2, ROWS, 256), bf16),
            pltpu.VMEM((EXT, 256), bf16),
            pltpu.VMEM((EXT, 256), bf16),
            pltpu.VMEM((3, 8, 16, 128), f32),
            pltpu.VMEM((3, 4, 16, 128), f32),
            pltpu.VMEM((8, 8, 128), f32),
            pltpu.VMEM((2, ROWS, 2048), f32),
            pltpu.VMEM((2, ROWS, 2048), f32),
            pltpu.VMEM((K, 2, ROWS, 2048), f32),
            dma((2,)), dma((1,)), dma((1,)),
            dma((K,)), dma((K, G)),
            dma((K,)), dma((K, G)),
            dma((K,)), dma((K, G, Z)),
            dma((K,)), dma((K, G, Z)),
            dma((3,)), dma((3,)),
            dma((3,)), dma((3,)),
        ],
        compiler_params=pltpu.CompilerParams(
            collective_id=0, has_side_effects=True, vmem_limit_bytes=48 << 20),
        cost_estimate=pl.CostEstimate(flops=13_000_000_000, bytes_accessed=8_000_000, transcendentals=0),
    )(vec, estimate, observed, weights))


def solution(mesh):
    return jax.shard_map(
        body,
        mesh=mesh,
        in_specs=(
            P("strip", None),
            P("frame", "strip", None),
            P("frame", "strip", None),
            P("frame", None),
            P("frame", None),
        ),
        out_specs=(P("strip", None), P("strip", None)),
        check_vma=False,
    )
```
